32 devices in a mesh: col: 4 (over y, x), tok: 8 (over z, core).
Axes of the slice: x: 2, y: 2, z: 4, core: 2. Of those that a mesh axis runs over, the one named last changes fastest.
Arguments:
- activations: bfloat16 [8192, 8192], P('tok', 'col'), may hold values from -6 to 6
Outputs:
- factor: float32 [8192, 8192], P(('col', 'tok'))
The draws below stay inside these ranges and needn't reach their ends.
All inputs are finite; a program needn't handle non-finite values.
Results may differ from the reference program's by a relative error of at most 0.0003.
Values may be sent and summed in bfloat16 or wider, within the bound.
No kernel may reach another device: no remote copies, remote signals or barrier semaphores. Data moves between devices by JAX's collectives and lax.ppermute only.
A program may use at most 128 MiB of HBM per device.

```python
import jax
import jax.numpy as jnp
from jax import lax

H = 8192
TOK_DEV = 1024
TOKENS = 8192
N_TOK = 8


def levels(stream_key, extent, shards, smallest, top_value):
    loudness = 1.0
    for position, blocks in shards:
        heights = jax.random.uniform(jax.random.fold_in(jax.random.fold_in(stream_key, 6), position), (blocks,), jnp.float32, smallest / len(shards), top_value / len(shards))
        loudness = loudness * jnp.repeat(jnp.exp(heights), extent[position] // blocks).reshape((-1,) + (1,) * (len(extent) - 1 - position))
    return loudness


def scatter_about(own_key, dims, scale, limit, cuts=(), dtype=jnp.bfloat16):
    entries = jax.random.normal(own_key, dims, jnp.float32) * scale
    if len(cuts) > 0:
        entries = levels(own_key, dims, cuts, -0.22, 0.18) * entries
    return jnp.clip(entries, min=-limit, max=limit).astype(dtype)


def setup_inputs(seed: int = 0) -> dict:
    streams_of = jax.random.split(jax.random.key(seed), 2)
    return {
        "activations": scatter_about(streams_of[0], (TOKENS, H), 1.0, 6.0, ((0, 8), (1, 4))),
    }


def reference(activations):
    token_blocks = activations.reshape(N_TOK, TOK_DEV, H)

    def accumulate(running_sum, token_block):
        values = token_block.astype(jnp.float32)
        product = jnp.dot(values.T, values, precision=lax.Precision.HIGHEST, preferred_element_type=jnp.float32)
        return running_sum + product, None

    start_sum = jnp.zeros((H, H), jnp.float32)
    token_sums, unused = lax.scan(accumulate, start_sum, token_blocks)
    return token_sums / jnp.float32(TOKENS)
```

```python
import jax
import jax.numpy as jnp
from jax import lax
from jax.experimental import pallas as pl
from jax.experimental.pallas import tpu as pltpu
from jax.sharding import PartitionSpec as P

POWER = 11
SHIFT = 11
SCALE_ROWS = 16
GROUP = 4
LANES = 128
VMEM_BYTES = 60 * 2**20


def encode(sums):
    top = jnp.max(jnp.abs(sums), axis=0, keepdims=True)
    top = jnp.maximum(top, 1e-30).astype(jnp.bfloat16).astype(jnp.float32)
    value = sums * (2.0**SHIFT / top)
    square = value * value
    fourth = square * square
    code = value * square * (fourth * fourth)
    scale = jnp.broadcast_to(top, (SCALE_ROWS, sums.shape[1]))
    return jnp.concatenate([code, scale], axis=0).astype(jnp.bfloat16)


def decode(block):
    wide = block.astype(jnp.float32)
    code, top = wide[:-SCALE_ROWS], wide[-SCALE_ROWS:]
    root = jnp.exp2(jnp.log2(jnp.abs(code)) * (1.0 / POWER))
    return jnp.where(code < 0, -root, root) * (top[:1] * 2.0**-SHIFT)


def dot(left, right):
    return jnp.dot(left, right, preferred_element_type=jnp.float32)


TOKEN = jax.ShapeDtypeStruct((8, LANES), jnp.float32)


class Sequence:
    def __init__(self):
        self.token = []

    def call(self, kernel, outs, operands, **settings):
        results = pl.pallas_call(
            kernel,
            out_shape=[*outs, TOKEN],
            in_specs=[pl.BlockSpec(memory_space=pltpu.HBM)] * (len(operands) + len(self.token)),
            out_specs=[pl.BlockSpec(memory_space=pltpu.HBM)] * (len(outs) + 1),
            cost_estimate=pl.CostEstimate(flops=1024, bytes_accessed=1024, transcendentals=0),
            compiler_params=pltpu.CompilerParams(vmem_limit_bytes=VMEM_BYTES),
            **settings,
        )(*operands, *self.token)
        self.token = [results[-1]]
        return results[:-1]

    def held(self, *values):
        outs = [jax.ShapeDtypeStruct(value.shape, value.dtype) for value in values]
        aliases = {index: index for index in range(len(values))}
        return self.call(lambda *refs: None, outs, values, input_output_aliases=aliases)

    def local(self, body, outs, *operands, into=None):
        count, tokens = len(operands), len(self.token)
        operands = [part if isinstance(part, tuple) else (part, part.shape, None) for part in operands]
        shapes = [out[0] if isinstance(out, tuple) else out for out in outs]
        saved = [out[1] if isinstance(out, tuple) else [out] for out in outs]
        slots = [part for parts in saved for part in parts]
        starts = [sum(map(len, saved[:index])) for index in range(len(saved))]
        numbered = [range(start, start + len(parts)) for start, parts in zip(starts, saved)]
        inputs = count + (into is not None) + tokens

        def kernel(*refs):
            sources, results, scratch = refs[:count], refs[inputs:], refs[inputs + len(outs) + 1 :]
            held_in, held_out, semaphores = scratch[:count], scratch[count:-1], scratch[-1]
            copies = [
                pltpu.make_async_copy(source.at[part[2]()] if part[2] else source, copy, semaphores.at[index])
                for index, (source, part, copy) in enumerate(zip(sources, operands, held_in))
            ]
            for copy in copies:
                copy.start()
            arrived, pending, free = set(), [], [[*numbers] for numbers in numbered]

            def load(index):
                if index not in arrived:
                    copies[index].wait()
                    arrived.add(index)
                return held_in[index]

            def save(index, value, *place):
                slot = free[index].pop(0)
                held_out[slot][...] = value
                target = results[index].at[place] if place else results[index]
                pending.append(pltpu.make_async_copy(held_out[slot], target, semaphores.at[count + slot]))
                pending[-1].start()

            body(load, save)
            for index in range(count):
                load(index)
            for copy in pending:
                copy.wait()

        return self.call(
            kernel,
            shapes,
            [*[part[0] for part in operands], *([] if into is None else [into])],
            scratch_shapes=[
                *[pltpu.VMEM(part[1], part[0].dtype) for part in operands],
                *[pltpu.VMEM(part.shape, part.dtype) for part in slots],
                pltpu.SemaphoreType.DMA((count + len(slots),)),
            ],
            input_output_aliases={} if into is None else {count: 0},
        )


def ring_place(index, cols):
    return index if index < cols // 2 else cols - 1 - (index - cols // 2)


def ring_permute(value, by):
    cols = lax.axis_size("col")
    pairs = [(ring_place(i, cols), ring_place((i + by) % cols, cols)) for i in range(cols)]
    return lax.ppermute(value, "col", pairs)


def narrow_shards(activations):
    block = activations.shape[1]
    toks, cols = lax.axis_size("tok"), lax.axis_size("col")
    col = lax.axis_index("col")
    total_tokens = activations.shape[0] * toks
    half = cols // 2

    def column(offset):
        position = jnp.where(col < half, col, cols - 1 - (col - half))
        position = (position + offset) % cols
        return jnp.where(position < half, position, cols - 1 - (position - half))

    factor_rows = jnp.zeros((block // toks, cols * block), jnp.float32)
    other = activations
    for offset in range(half + 1):
        tile = lax.dot_general(activations, other, (((0,), (0,)), ((), ())), preferred_element_type=jnp.float32)
        rows = lax.psum_scatter(tile, "tok", scatter_dimension=0, tiled=True) / jnp.float32(total_tokens)
        factor_rows = lax.dynamic_update_slice(factor_rows, rows, (0, column(offset) * block))
        if 0 < offset < half:
            turned = lax.all_to_all(rows, "tok", split_axis=1, concat_axis=0, tiled=True).T
            factor_rows = lax.dynamic_update_slice(
                factor_rows, ring_permute(turned, offset), (0, column(-offset) * block)
            )
        if offset < half:
            other = ring_permute(other, -1)
    return factor_rows


def shards(activations):
    tokens, block = activations.shape
    toks = lax.axis_size("tok")
    cols = lax.axis_size("col")
    share = block // toks
    width = 2 * share
    if share % LANES:
        return narrow_shards(activations)
    groups = toks // GROUP
    half = cols // 2
    scale = 1.0 / (tokens * toks)
    steps = range(groups)
    sent_first = [*range(1, groups), 0]

    def along_tok(value, step, other_side=0, other_core=0):
        def target(index):
            return (index + GROUP * step) % toks ^ (2 * other_side + other_core)

        return lax.ppermute(value, "tok", [(i, target(i)) for i in range(toks)])

    def ring_column(offset):
        col = lax.axis_index("col")
        position = jnp.where(col < half, col, cols - 1 - (col - half))
        position = lax.rem(position + offset + cols, cols)
        return jnp.where(position < half, position, cols - 1 - (position - half))

    def feature_start(step, which):
        tok = lax.axis_index("tok")
        group, side = lax.div(tok, GROUP), lax.div(lax.rem(tok, GROUP), 2)
        side = side if which == 0 else 1 - side
        return (lax.rem(group + step, groups) * 2 + side) * width

    def core_start(other_core=0):
        core = lax.rem(lax.axis_index("tok"), 2)
        return (core if other_core == 0 else 1 - core) * share

    names = [(step, which) for which in range(2) for step in sent_first]
    first, second = names[:groups], names[groups:]
    shape = jax.ShapeDtypeStruct
    order = Sequence()
    rows_shape = shape((share, cols * block), jnp.float32)

    def columns(array, start, count):
        return (array, (tokens, count), lambda: (slice(None), pl.ds(pl.multiple_of(start(), LANES), count)))

    def side_features(which, apart):
        def body(load, save):
            for index in range(groups):
                if apart:
                    save(index, load(index)[...])
                else:
                    save(0, load(index)[...], slice(None), pl.ds(index * width, width))

        parts = [columns(activations, lambda step=step: feature_start(step, which), width) for step in sent_first]
        piece = shape((tokens, width), jnp.bfloat16)
        if apart:
            return list(order.local(body, [piece] * groups, *parts))
        return order.local(body, [(shape((tokens, groups * width), jnp.bfloat16), [piece] * groups)], *parts)[0]

    own = [None, side_features(1, False)]
    mate = along_tok(activations, 0, 0, 1)
    near = [along_tok(own[1], 0, 1), [None] * groups]
    near_mate = [None, [None] * groups]
    own[0] = side_features(0, True)

    def at(source, step, start, count):
        index = sent_first.index(step)
        if isinstance(source, list):
            return columns(source[index], start, count)
        return columns(source, lambda: index * width + start(), count)

    def row_part(source, step):
        if source is mate:
            return columns(mate, lambda: feature_start(step, 0) + core_start(), share)
        return at(source, step, core_start, share)

    def row_operand(sources, step):
        count = len(sources)

        def body(load, save):
            save(0, jnp.concatenate([load(index)[...].T for index in range(count)], axis=1))

        out = shape((share, count * tokens), jnp.bfloat16)
        return order.local(body, [out], *[row_part(source, step) for source in sources])[0]

    def operands(rows, blocks):
        arrays, table = [*rows], {}

        for step, which in blocks:
            parts = [at(source[which], step, lambda: 0, width) for source in (own, near, near_mate)]
            parts.insert(1, columns(mate, lambda step=step, which=which: feature_start(step, which), width))
            table[step, which] = range(len(arrays), len(arrays) + 4)
            arrays += parts
        return arrays, table

    def product(load, rows, table, name):
        total = None
        each = 4 // len(rows)
        for number, slot in enumerate(table[name]):
            left = load(number // each)[:, (number % each) * tokens : (number % each + 1) * tokens]
            term = dot(left, load(slot)[...])
            total = term if total is None else total + term
        return total

    def own_sums(rows, blocks):
        arrays, table = operands(rows, blocks)

        def body(load, save):
            for index, name in enumerate(blocks):
                save(0, product(load, rows, table, name), slice(None), pl.ds(index * width, width))

        value_shape = shape((share, width), jnp.float32)
        out = (shape((share, len(blocks) * width), jnp.float32), [value_shape] * len(blocks))
        return order.local(body, [out], *arrays)[0]

    def code_of(blocks):
        return shape((share + SCALE_ROWS, len(blocks) * width), jnp.bfloat16)

    def partial_sums(rows, blocks):
        arrays, table = operands(rows, blocks)

        def body(load, save):
            for index, name in enumerate(blocks):
                code = encode(product(load, rows, table, name))
                save(0, code, slice(None), pl.ds(index * width, width))

        piece = shape((share + SCALE_ROWS, width), jnp.bfloat16)
        return order.local(body, [(code_of(blocks), [piece] * len(blocks))], *arrays)[0]

    def totals(offset, rows, blocks, arrived, into, ready=None):
        arrays, table = operands(rows, blocks) if ready is None else ([ready], None)
        mirrored = 0 < offset < half
        place = {}
        for back, codes in enumerate(arrived, 1):
            for code, code_blocks in codes:
                arrays.append(code)
                for index, (step, which) in enumerate(code_blocks):
                    place[back, ((step - back) % groups, which)] = (len(arrays) - 1, index * width)

        def body(load, save):
            for index, name in enumerate(blocks):
                if ready is None:
                    value = product(load, rows, table, name)
                else:
                    value = load(0)[:, index * width : (index + 1) * width]
                for back in range(1, groups):
                    slot, start = place[back, name]
                    value = value + decode(load(slot)[:, start : start + width])
                if offset == 0:
                    start = ring_column(0) * block + feature_start(*name)
                    save(0, value * scale, slice(None), pl.ds(pl.multiple_of(start, LANES), width))
                else:
                    save(0, encode(value), slice(None), pl.ds(index * width, width))
                    if mirrored:
                        save(1, value, slice(None), pl.ds(index * width, width))

        value_shape = shape((share, width), jnp.float32)
        if offset == 0:
            outs = [(rows_shape, [value_shape] * len(blocks))]
        else:
            outs = [(code_of(blocks), [shape((share + SCALE_ROWS, width), jnp.bfloat16)] * len(blocks))]
        if mirrored:
            outs.append((shape((share, len(blocks) * width), jnp.float32), [value_shape] * len(blocks)))
        return order.local(body, outs, *arrays, into=into)

    def turned_pieces(value):
        def body(load, save):
            for index in range(len(names)):
                turned = load(0)[:, index * width : (index + 1) * width].T
                first_core = jnp.full((1, share), core_start(), jnp.int32) == 0
                one, two = turned[:share], turned[share:]
                same = jnp.where(first_core, one, two)
                other = jnp.where(first_core, two, one)
                save(index, encode(jnp.concatenate([same, other], axis=0)))

        return order.local(body, [shape((width + SCALE_ROWS, share), jnp.bfloat16)] * len(names), value)

    def for_mate(pieces):
        def body(load, save):
            parts = [load(index)[share:] for index in range(len(names))]
            save(0, jnp.concatenate(parts, axis=0))

        return order.local(
            body, [shape((len(names) * (share + SCALE_ROWS), share), jnp.bfloat16)], *pieces
        )[0]

    def place_returned(offset, code, blocks, into):
        def body(load, save):
            for index, name in enumerate(blocks):
                value = decode(load(0)[:, index * width : (index + 1) * width]) * scale
                start = ring_column(offset) * block + feature_start(*name)
                save(0, value, slice(None), pl.ds(pl.multiple_of(start, LANES), width))

        value_shape = shape((share, width), jnp.float32)
        return order.local(body, [(rows_shape, [value_shape] * len(blocks))], code, into=into)[0]

    def place_mirrored(offset, pieces, from_mate, into):
        def body(load, save):
            for index, (step, which) in enumerate(names):
                rows = share + SCALE_ROWS
                piece = load(index)
                mine = jnp.concatenate([piece[:share], piece[width:]], axis=0)
                for other_core, code in enumerate((mine, load(len(names))[index * rows : (index + 1) * rows])):
                    start = feature_start((groups - step) % groups, which) + core_start(other_core)
                    start = ring_column(-offset) * block + start
                    save(0, decode(code) * scale, slice(None), pl.ds(pl.multiple_of(start, LANES), share))

        value_shape = shape((share, share), jnp.float32)
        return order.local(
            body, [(rows_shape, [value_shape] * (2 * len(names)))], *pieces, from_mate, into=into
        )[0]

    left = [{step: [] for step in steps} for offset in range(half + 1)]
    sent_steps = range(1, groups)

    def start_rows(pair, turn):
        backward = {}
        for step in sent_steps:
            rows = row_operand(pair, step)
            left[0][step].append(rows)
            for offset in range(1, half):
                rows = ring_permute(rows, 1)
                left[offset][step].append(rows)
            if turn:
                backward[step] = ring_permute(left[0][step][-1], -1)
        return backward

    def relayed(backward):
        for hop in range(1, half):
            for step in sent_steps:
                backward[step] = ring_permute(order.held(backward[step])[0], -1)
        return backward

    def send(offset, blocks):
        return [(along_tok(partial_sums(left[offset][step], blocks), step), blocks) for step in sent_steps]

    def settled(sent):
        return [(order.held(code)[0], blocks) for code, blocks in sent]

    def settle(offset):
        for step in sent_steps:
            left[offset][step][-1] = order.held(left[offset][step][-1])[0]

    def computed(offset, blocks):
        return [partial_sums(left[offset][step], blocks) for step in sent_steps]

    def sent(codes, blocks):
        return [(along_tok(order.held(code)[0], step), blocks) for step, code in zip(sent_steps, codes)]

    inner = range(1, half)
    sums = {}
    def from_near(index):
        near[1][index] = order.held(near[1][index])[0]
        near_mate[1][index] = along_tok(near[1][index], 0, 0, 1)

    def to_near(index):
        near[1][index] = along_tok(own[0][index], 0, 1)

    backward = start_rows([own[0], mate], True)
    for offset in inner:
        settle(offset)
    backward = relayed(backward)
    near[0], *own[0] = order.held(near[0], *own[0])
    near_mate[0] = along_tok(near[0], 0, 0, 1)
    to_near(0)
    start_rows([near[0], near_mate[0]], False)
    sums[0, 0] = send(0, first)
    here = row_operand([own[0], mate, near[0], near_mate[0]], 0)
    left[0][0] = [here]
    for offset in inner:
        left[offset][0] = [ring_permute(here, offset)]
    opposite = ring_permute(here, -1)
    for step in sent_steps:
        left[half][step].append(order.held(backward[step])[0])
    from_near(0)
    for offset in inner:
        settle(offset)
    for step in sent_steps:
        left[half][step].append(ring_permute(left[half - 1][step][-1], 1))
    for index in range(1, groups):
        own[0][index] = order.held(own[0][index])[0]
        to_near(index)
    codes = {offset: computed(offset, first) for offset in inner}
    sums[0, 0] = settled(sums[0, 0])
    for offset in inner:
        sums[offset, 0] = sent(codes[offset], first)
    factor_rows = totals(0, left[0][0], first, [[part] for part in sums[0, 0]], None)[0]
    for step in sent_steps:
        left[half][step][-1] = order.held(left[half][step][-1])[0]
    codes = computed(half, first)
    for offset in inner:
        sums[offset, 0] = settled(sums[offset, 0])
    for index in range(1, groups):
        from_near(index)
    sums[half, 0] = sent(codes, first)
    for offset in inner:
        sums[offset, 1] = send(offset, second)
    codes = computed(half, second)
    sums[half, 0] = settled(sums[half, 0])
    for hop in range(1, half):
        opposite = ring_permute(order.held(opposite)[0], -1)
    left[half][0] = [opposite]
    last = computed(0, second)
    ready = own_sums(left[0][0], second)
    for offset in inner:
        left[offset][0] = order.held(*left[offset][0])
    for offset in inner:
        sums[offset, 1] = settled(sums[offset, 1])
    sums[half, 1] = sent(codes, second)

    turned, returned, values = {}, {}, {}
    for offset in inner:
        parts = [list(pair) for pair in zip(sums[offset, 0], sums[offset, 1])]
        code, values[offset] = totals(offset, left[offset][0], names, parts, None)
        returned[offset] = ring_permute(code, -offset)
    for offset in inner:
        pieces = turned_pieces(values[offset])
        turned[offset] = [
            piece if name == (0, 0) else along_tok(piece, *name) for name, piece in zip(names, pieces)
        ]
    returned[half] = []
    for which, blocks in enumerate((first, second)):
        if which:
            sums[half, 1] = settled(sums[half, 1])
            for offset in inner:
                inside = names.index((0, 1))
                turned[offset][inside] = order.held(turned[offset][inside])[0]
        code = totals(half, left[half][0], blocks, [[part] for part in sums[half, which]], None)[0]
        returned[half].append(ring_permute(code, -half))
    for offset in inner:
        turned[offset] = order.held(*turned[offset])
    sums[0, 1] = sent(last, second)
    for offset in inner:
        turned[offset] = [*turned[offset], along_tok(for_mate(turned[offset]), 0, 0, 1)]
    for offset in inner:
        factor_rows = place_returned(offset, returned[offset], names, factor_rows)
    for blocks, code in zip((first, second), returned[half]):
        factor_rows = place_returned(half, code, blocks, factor_rows)
    for offset in inner:
        factor_rows = place_mirrored(offset, turned[offset][:-1], turned[offset][-1], factor_rows)
    return totals(0, None, second, [[part] for part in sums[0, 1]], factor_rows, ready)[0]


def solution(mesh):
    in_specs = (P("tok", "col"),)
    out_specs = P(("col", "tok"), None)
    return jax.shard_map(shards, mesh=mesh, in_specs=in_specs, out_specs=out_specs, check_vma=False)
```
